256 devices in a mesh: feat: 32 (over x, y, core), batch: 8 (over z).
Axes of the slice: x: 4, y: 4, z: 8, core: 2. Of those that a mesh axis runs over, the one named last changes fastest.
Arguments:
- node_features: bfloat16 [768, 32768], P('feat'), may hold values from -6 to 6
- first_weight: bfloat16 [768, 2, 1024], P('feat'), may hold values from -0.15625 to 0.15625
- second_weight: bfloat16 [2048, 1024], replicated, may hold values from -0.125 to 0.125
- target_nodes: int32 [8, 2048], P('batch'), may hold values from 0 to 32767
- outer_nodes: int32 [8, 2048, 16], P('batch'), may hold values from 0 to 32767
- outer_counts: int32 [8, 2048], P('batch'), may hold values from 1 to 16
- inner_nodes: int32 [8, 1024, 8], P('batch', 'feat'), may hold values from 0 to 63
- inner_counts: int32 [8, 1024], P('batch', 'feat'), may hold values from 1 to 8
- cotangent: bfloat16 [8, 1024, 1024], P('batch', 'feat'), may hold values from -6 to 6
Outputs:
- output_rows: bfloat16 [8, 1024, 1024], P('batch', 'feat')
- grad_second: float32 [2048, 1024], P(('feat', 'batch'))
- grad_first: float32 [768, 2, 1024], P('feat')
The draws below stay inside these ranges and needn't reach their ends.
All inputs are finite; a program needn't handle non-finite values.
Results may differ from the reference program's by a relative error of at most 0.02.
Values may be sent and summed in bfloat16 or wider, within the bound.
No kernel may reach another device: no remote copies, remote signals or barrier semaphores. Data moves between devices by JAX's collectives and lax.ppermute only.
A program may use at most 128 MiB of HBM per device.

```python
import jax
import jax.numpy as jnp
from jax import lax

D = 768
H = 1024
FAN1 = 16
FAN2 = 8
L1_DEV = 64
T_DEV = 32
GROUPS = 8
GROUP_ROWS = 2048
OWN2 = 1024
NODES = 32768
N_FEAT = 32


def plant(array, rng, low, largest):
    extent = array.shape
    spot = [jax.random.randint(jax.random.fold_in(rng, axis), (), 0, extent[axis]) for axis in range(len(extent))]
    array = array.at[tuple(spot)].set(low)
    longest = extent.index(max(extent))
    spot[longest] = (spot[longest] + 1) % extent[longest]
    return array.at[tuple(spot)].set(largest)


def shard_levels(key, extent, pieces, least, top_value):
    def one(dim, parts):
        heights = jax.random.uniform(jax.random.fold_in(jax.random.fold_in(key, 6), dim), (parts,), jnp.float32, least / len(pieces), top_value / len(pieces))
        return jnp.repeat(jnp.exp(heights), extent[dim] // parts).reshape((-1,) + (1,) * (len(extent) - dim - 1))

    factor_of = one(*pieces[0])
    for cut in pieces[1:]:
        factor_of = factor_of * one(*cut)
    return factor_of


def noise(stream_key, shape, width, reach, split=(), held_as=jnp.bfloat16):
    entries = width * jax.random.normal(stream_key, shape, jnp.float32)
    if split:
        entries = entries * shard_levels(stream_key, shape, split, -0.22, 0.18)
    return jnp.clip(entries, -reach, reach).astype(held_as)


def setup_inputs(seed: int = 0) -> dict:
    streams_of = jax.random.split(jax.random.key(seed), 10)
    node_features = noise(streams_of[0], (D, NODES), 1.0, 6.0, ((0, 32),))
    first_weight = noise(streams_of[1], (D, 2, H), (2 * D) ** -0.5, 0.15625, ((0, 32),))
    second_weight = noise(streams_of[2], (2 * H, H), (2 * H) ** -0.5, 0.125)
    target_nodes = plant(jax.random.randint(streams_of[3], (GROUPS, GROUP_ROWS), 0, NODES), jax.random.fold_in(streams_of[3], 1), 0, NODES - 1).astype(jnp.int32)
    outer_nodes = plant(jax.random.randint(streams_of[4], (GROUPS, GROUP_ROWS, FAN1), 0, NODES), jax.random.fold_in(streams_of[4], 1), 0, NODES - 1).astype(jnp.int32)
    outer_counts = plant(jax.random.randint(streams_of[5], (GROUPS, GROUP_ROWS), 1, FAN1 + 1), jax.random.fold_in(streams_of[5], 1), 1, FAN1).astype(jnp.int32)
    inner_nodes = plant(jax.random.randint(streams_of[6], (GROUPS, OWN2, FAN2), 0, L1_DEV), jax.random.fold_in(streams_of[6], 1), 0, L1_DEV - 1).astype(jnp.int32)
    inner_counts = plant(jax.random.randint(streams_of[7], (GROUPS, OWN2), 1, FAN2 + 1), jax.random.fold_in(streams_of[7], 1), 1, FAN2).astype(jnp.int32)
    cotangent = noise(streams_of[8], (GROUPS, OWN2, H), 1.0, 6.0, ((0, 8), (1, 32)))
    return {"node_features": node_features, "first_weight": first_weight, "second_weight": second_weight, "target_nodes": target_nodes, "outer_nodes": outer_nodes, "outer_counts": outer_counts, "inner_nodes": inner_nodes, "inner_counts": inner_counts, "cotangent": cotangent}


def silu_slope(values):
    sig = jax.nn.sigmoid(values)
    return sig * (1.0 + values * (1.0 - sig))


def owner_pass(hidden_rows, pre_rows, inner, inner_cnt, upstream_gradient, second_weight):
    slots = jnp.arange(FAN2, dtype=jnp.int32)
    valid_mask = (slots[None, :] < inner_cnt[:, None]).astype(jnp.float32)
    columns = jnp.arange(L1_DEV, dtype=jnp.int32)
    tally = jnp.sum((inner[:, :, None] == columns[None, None, :]).astype(jnp.float32) * valid_mask[:, :, None], axis=1)
    divisor = inner_cnt.astype(jnp.float32)[:, None]
    mean_rows = (jnp.dot(tally, hidden_rows.astype(jnp.float32), precision=lax.Precision.HIGHEST) / divisor).astype(jnp.bfloat16)
    joined = jnp.concatenate([hidden_rows[:T_DEV], mean_rows], axis=1)
    output = jnp.dot(joined, second_weight, preferred_element_type=jnp.float32).astype(jnp.bfloat16)
    weight_gradient = lax.dot_general(joined, upstream_gradient, (((0,), (0,)), ((), ())), preferred_element_type=jnp.float32)
    grad_joined = lax.dot_general(upstream_gradient, second_weight, (((1,), (1,)), ((), ())), preferred_element_type=jnp.float32)
    spread = lax.dot_general(tally, grad_joined[:, H:] / divisor, (((0,), (0,)), ((), ())), precision=lax.Precision.HIGHEST)
    grad_hidden = spread + jnp.pad(grad_joined[:, :H], ((0, L1_DEV - T_DEV), (0, 0)))
    grad_pre = (grad_hidden * silu_slope(pre_rows)).astype(jnp.bfloat16)
    return output, weight_gradient, grad_pre


def reference(node_features, first_weight, second_weight, target_nodes, outer_nodes, outer_counts, inner_nodes, inner_counts, cotangent):
    def group_step(totals, group_args):
        target_indices, outer, outer_cnt, inner, inner_cnt, upstream_gradient = group_args
        self_part = node_features[:, target_indices]
        neighbour_indices = node_features[:, outer].astype(jnp.float32)
        slots = jnp.arange(FAN1, dtype=jnp.int32)
        valid_mask = (slots[None, :] < outer_cnt[:, None]).astype(jnp.float32)
        averaged = (jnp.sum(neighbour_indices * valid_mask[None], axis=2) / outer_cnt.astype(jnp.float32)[None, :]).astype(jnp.bfloat16)
        stacked = jnp.stack([self_part, averaged], axis=1)
        pre = lax.dot_general(stacked.astype(jnp.float32), first_weight.astype(jnp.float32), (((0, 1), (0, 1)), ((), ())), precision=lax.Precision.HIGHEST)
        hidden = jax.nn.silu(pre).astype(jnp.bfloat16)

        def owner_step(grad_acc, owner_args):
            hid, prr, inn, icn, gro = owner_args
            output, weight_gradient, grad_pre = owner_pass(hid, prr, inn, icn, gro, second_weight)
            return grad_acc + weight_gradient, (output, grad_pre)

        owner_args = (hidden.reshape(N_FEAT, L1_DEV, H), pre.reshape(N_FEAT, L1_DEV, H), inner.reshape(N_FEAT, T_DEV, FAN2), inner_cnt.reshape(N_FEAT, T_DEV), upstream_gradient.reshape(N_FEAT, T_DEV, H))
        grad_second, (outputs, grad_pre) = lax.scan(owner_step, totals[0], owner_args)
        grad_first = lax.dot_general(stacked.astype(jnp.float32), grad_pre.reshape(GROUP_ROWS, H).astype(jnp.float32), (((2,), (0,)), ((), ())), precision=lax.Precision.HIGHEST)
        return (grad_second, totals[1] + grad_first), outputs.reshape(OWN2, H)

    start = (jnp.zeros((2 * H, H), jnp.float32), jnp.zeros((D, 2, H), jnp.float32))
    (grad_second, grad_first), output_rows = lax.scan(group_step, start, (target_nodes, outer_nodes, outer_counts, inner_nodes, inner_counts, cotangent))
    return output_rows, grad_second, grad_first
```

```python
import jax
import jax.numpy as jnp
from jax import lax
from jax.experimental import pallas as pl
from jax.experimental.pallas import tpu as pltpu
from jax.sharding import Mesh, PartitionSpec as P

BF16 = jnp.bfloat16
F32 = jnp.float32
LANES = 128


def gather_kernel(slots, owners, owners_y, owner_rows, slice_width, table_rows):
    def kernel(place_ref, index_ref, target_ref, own_ref, other_ref, count_ref, out_ref, relative_ref, table, rows):
        core, here = place_ref[0], place_ref[1]
        group_rows = owners * 2 * owner_rows
        lane = lax.broadcasted_iota(jnp.int32, (1, LANES), 1)
        is_self = (lane // slice_width) % 2 == 0
        tail = jnp.zeros((LANES - 4 * slice_width, LANES), F32)

        def turn(step, carry):
            for part in range(2):
                start = pl.multiple_of((step * 2 + part) * LANES, LANES)
                own = own_ref[:, pl.ds(start, LANES)].astype(F32)
                other = other_ref[:, pl.ds(start, LANES)].astype(F32)
                first = jnp.where(core == 0, own, other)
                second = jnp.where(core == 0, other, own)
                block = jnp.concatenate([first, first, second, second, tail], axis=0)
                table[pl.ds(start, LANES), :] = block.T
            return carry

        lax.fori_loop(0, table_rows // (2 * LANES), turn, 0)
        table[pl.ds(table_rows, 8), :] = jnp.zeros((8, LANES), F32)

        unroll = 8
        chunks = owner_rows // unroll

        def look_up(step, carry):
            owner = step // chunks
            source = (owner * 2 + core) * owner_rows + (step % chunks) * unroll
            for part in range(unroll):
                terms = [
                    table[pl.ds(index_ref[slot * group_rows + source + part], 1), :] for slot in range(slots)
                ]
                while len(terms) > 1:
                    terms = [a + b for a, b in zip(terms[::2], terms[1::2])]
                self_row = table[pl.ds(target_ref[source + part], 1), :]
                rows[pl.ds(step * unroll + part, 1), :] = jnp.where(is_self, self_row, terms[0])
            return carry

        lax.fori_loop(0, owners * chunks, look_up, 0)

        for owner in range(owners):
            source = pl.multiple_of((owner * 2 + core) * owner_rows, owner_rows)
            counts = jnp.broadcast_to(count_ref[pl.ds(source, owner_rows), :], (owner_rows, LANES))
            divisor = jnp.where(jnp.broadcast_to(is_self, (owner_rows, LANES)), 1.0, counts)
            values = rows[pl.ds(owner * owner_rows, owner_rows), :] / divisor
            values = values[:, : 4 * slice_width].astype(BF16)
            out_ref[owner] = values
            turn_y = lax.rem(owner % owners_y - here + owners_y, owners_y)
            relative_ref[turn_y, pl.ds(owner // owners_y * owner_rows, owner_rows), :] = values

    smem = pl.BlockSpec(memory_space=pltpu.SMEM)
    vmem = pl.BlockSpec(memory_space=pltpu.VMEM)
    return pl.pallas_call(
        kernel,
        out_shape=(
            jax.ShapeDtypeStruct((owners, owner_rows, 4 * slice_width), BF16),
            jax.ShapeDtypeStruct((owners_y, owners // owners_y * owner_rows, 4 * slice_width), BF16),
        ),
        in_specs=[smem, smem, smem, vmem, vmem, vmem],
        out_specs=(vmem, vmem),
        scratch_shapes=[
            pltpu.VMEM((table_rows + 8, LANES), F32),
            pltpu.VMEM((owners * owner_rows, LANES), F32),
        ],
        compiler_params=pltpu.CompilerParams(vmem_limit_bytes=48 << 20),
        cost_estimate=pl.CostEstimate(flops=50_000_000, bytes_accessed=100_000_000, transcendentals=0),
        name="gather_mean",
    )


def silu_slope(values):
    sig = jax.nn.sigmoid(values)
    return sig * (1.0 + values * (1.0 - sig))


def swap(values):
    return lax.ppermute(values, "core", [(0, 1), (1, 0)])


def exchange(values, axis):
    return lax.all_to_all(values, axis, split_axis=0, concat_axis=0, tiled=True)


def turn_blocks(blocks, axis):
    n = len(blocks)
    here = lax.axis_index(axis)
    got = [blocks[0]] + [lax.ppermute(blocks[k], axis, [(i, (i + k) % n) for i in range(n)]) for k in range(1, n)]
    return got, lambda got: jnp.stack(
        [lax.dynamic_index_in_dim(jnp.stack(got), (here - j) % n, 0, keepdims=False) for j in range(n)]
    )


def body(
    node_features,
    first_weight,
    second_weight,
    target_nodes,
    outer_nodes,
    outer_counts,
    inner_nodes,
    inner_counts,
    cotangent,
):
    nx, ny, nb = lax.axis_size("x"), lax.axis_size("y"), lax.axis_size("batch")
    core = lax.axis_index("core")
    slice_width, nodes = node_features.shape
    width = second_weight.shape[1]
    half = width // 2
    group_rows, slots = outer_nodes.shape[1:]
    owner_rows = group_rows // (nx * ny * 2)
    second_rows, fan_inner = inner_nodes.shape[1:]
    both = 2 * slice_width
    upstream = cotangent[0]

    weight = first_weight.transpose(1, 0, 2).reshape(both, width)
    kept = lax.dynamic_slice_in_dim(weight, core * half, half, axis=1)
    sent = swap(lax.dynamic_slice_in_dim(weight, (1 - core) * half, half, axis=1))
    pair = jnp.concatenate([jnp.where(core == 0, kept, sent), jnp.where(core == 0, sent, kept)], axis=0)
    weight_mine = exchange(jnp.broadcast_to(pair[None], (nx * ny,) + pair.shape), ("x", "y"))
    weight_mine = weight_mine.reshape(nx * ny * 2 * both, half)

    counts = outer_counts[0]
    live = jnp.arange(slots, dtype=jnp.int32)[:, None] < counts[None, :]
    index = jnp.where(live, outer_nodes[0].T, nodes).reshape(-1)
    other_features = swap(node_features)
    stacked, relative = gather_kernel(slots, nx * ny, ny, owner_rows, slice_width, nodes)(
        jnp.stack([core, lax.axis_index("y")]).astype(jnp.int32),
        index,
        target_nodes[0],
        node_features,
        other_features,
        counts.astype(F32)[:, None],
    )
    stacked, weight_mine = lax.optimization_barrier((stacked, weight_mine))
    weight_other = swap(weight_mine)
    owned = exchange(stacked, ("x", "y"))
    got, in_order = turn_blocks([relative[k] for k in range(ny)], "y")
    got[1], late_upstream = lax.optimization_barrier((got[1], upstream))
    along_y = in_order(got)
    owned = owned.transpose(1, 0, 2).reshape(owner_rows, nx * ny * 2 * both)
    pre_mine = jnp.dot(owned, weight_mine, preferred_element_type=F32)
    pre_other = jnp.dot(owned, weight_other, preferred_element_type=F32)
    pre = jnp.concatenate(
        [jnp.where(core == 0, pre_mine, pre_other), jnp.where(core == 0, pre_other, pre_mine)], axis=1
    )
    hidden = jax.nn.silu(pre).astype(BF16)

    inner = inner_nodes[0]
    inner_cnt = inner_counts[0]
    inner_live = (jnp.arange(fan_inner, dtype=jnp.int32)[None, :] < inner_cnt[:, None]).astype(F32)
    columns = jnp.arange(owner_rows, dtype=jnp.int32)
    tally = jnp.sum((inner[:, :, None] == columns[None, None, :]).astype(F32) * inner_live[:, :, None], axis=1)
    divisor = inner_cnt.astype(F32)[:, None]
    mean_rows = (jnp.dot(tally.astype(BF16), hidden, preferred_element_type=F32) / divisor).astype(BF16)
    joined = jnp.concatenate([hidden[:second_rows], mean_rows], axis=1)
    output = jnp.dot(joined, second_weight, preferred_element_type=F32).astype(BF16)
    grad_joined = lax.dot_general(late_upstream, second_weight, (((1,), (1,)), ((), ())), preferred_element_type=F32)
    spread = lax.dot_general(
        tally, grad_joined[:, width:] / divisor, (((0,), (0,)), ((), ())), precision=lax.Precision.HIGHEST
    )
    grad_hidden = spread + jnp.pad(grad_joined[:, :width], ((0, owner_rows - second_rows), (0, 0)))
    grad_pre = (grad_hidden * silu_slope(pre)).astype(BF16)

    chunk = 2 * width // nx
    columns_x = joined.reshape(second_rows, nx, chunk).transpose(1, 0, 2)
    columns_x = jnp.concatenate([columns_x[:, : second_rows // 2], columns_x[:, second_rows // 2 :]], axis=2)
    common = jnp.concatenate([grad_pre, upstream], axis=0)
    message = jnp.concatenate([jnp.broadcast_to(common[None], (nx,) + common.shape), columns_x], axis=1)
    message = exchange(message, "x")
    grad_pre_x = message[:, :owner_rows].reshape(nx * owner_rows, width)
    upstream_x = message[:, owner_rows : owner_rows + second_rows].reshape(nx * second_rows, width)
    columns_x = message[:, owner_rows + second_rows :]
    columns_x = jnp.concatenate([columns_x[:, :, :chunk], columns_x[:, :, chunk:]], axis=1)
    columns_x = columns_x.reshape(nx * second_rows, chunk)
    first_terms = lax.dot_general(
        along_y, grad_pre_x, (((1,), (0,)), ((), ())), preferred_element_type=F32
    ).reshape(ny, 2, both, width)

    kept = lax.dynamic_index_in_dim(first_terms, core, 1, keepdims=False)
    sent = swap(lax.dynamic_index_in_dim(first_terms, 1 - core, 1, keepdims=False).astype(BF16))
    piece = width // nb
    first_terms = (kept + sent.astype(F32)).astype(BF16).reshape(ny, both, nb, piece).transpose(0, 2, 1, 3)
    first_terms, columns_x = lax.optimization_barrier((first_terms.reshape(ny * nb, both, piece), columns_x))
    first_terms = exchange(first_terms, ("y", "batch"))
    first_piece = jnp.sum(first_terms.astype(F32), axis=0).astype(BF16)

    second_terms = lax.dot_general(
        columns_x, upstream_x, (((0,), (0,)), ((), ())), preferred_element_type=F32
    ).reshape(ny, 2, -1, width)
    kept = lax.dynamic_index_in_dim(second_terms, core, 1, keepdims=False)
    sent = swap(lax.dynamic_index_in_dim(second_terms, 1 - core, 1, keepdims=False).astype(BF16))
    second_terms = (kept + sent.astype(F32)).astype(BF16)
    here = lax.axis_index("y")
    got, _ = turn_blocks(
        [lax.dynamic_index_in_dim(second_terms, (here + k) % ny, 0, keepdims=False) for k in range(ny)], "y"
    )
    second_terms = sum(block.astype(F32) for block in got).astype(BF16)
    second_terms = second_terms.reshape(nb, -1, nb, piece).transpose(0, 2, 1, 3).reshape(nb, -1, piece)
    message = jnp.concatenate([jnp.broadcast_to(first_piece[None], (nb, both, piece)), second_terms], axis=1)
    message = exchange(message, "batch")
    grad_second = jnp.sum(message[:, both:].astype(F32), axis=0)
    grad_second = grad_second.reshape(nb, -1, piece).transpose(1, 0, 2).reshape(-1, width)
    grad_first = message[:, :both].reshape(nb, 2, slice_width, piece)
    grad_first = grad_first.transpose(2, 1, 0, 3).reshape(slice_width, 2, width)
    return (output[None], grad_second, grad_first.astype(F32))


def solution(mesh):
    feat, batch = mesh.devices.shape
    fine = Mesh(mesh.devices.reshape(4, feat // 8, 2, batch), ("x", "y", "core", "batch"))
    f = ("x", "y", "core")
    in_specs = (
        P(f, None),
        P(f, None, None),
        P(),
        P("batch", None),
        P("batch", None, None),
        P("batch", None),
        P("batch", f, None),
        P("batch", f),
        P("batch", f, None),
    )
    out_specs = (P("batch", f, None), P(("x", "y", "core", "batch"), None), P(f, None, None))
    return jax.shard_map(body, mesh=fine, in_specs=in_specs, out_specs=out_specs, check_vma=False)
```

```python
import jax
import jax.numpy as jnp
from jax import lax
from jax.experimental import pallas as pl
from jax.experimental.pallas import tpu as pltpu
from jax.sharding import Mesh, PartitionSpec as P

BF16 = jnp.bfloat16
F32 = jnp.float32
LANES = 128


def gather_kernel(slots, owners, owners_y, owner_rows, slice_width, table_rows, width):
    def kernel(place_ref, index_ref, target_ref, count_ref, own_ref, other_ref, out_ref, relative_ref, table, rows):
        core, here = place_ref[0], place_ref[1]
        group_rows = owners * 2 * owner_rows
        lane = lax.broadcasted_iota(jnp.int32, (1, LANES), 1)
        is_self = (lane // slice_width) % 2 == 0
        blocks = 16
        span = blocks * LANES
        tail = jnp.zeros((LANES - 4 * slice_width, span), F32)

        def turn(step, carry):
            start = pl.multiple_of(step * span, span)
            own = own_ref[:, pl.ds(start, span)].astype(F32)
            other = other_ref[:, pl.ds(start, span)].astype(F32)
            first = jnp.where(core == 0, own, other)
            second = jnp.where(core == 0, other, own)
            wide = jnp.concatenate([first, first, second, second, tail], axis=0).astype(BF16)
            for part in range(blocks):
                block = wide[:, part * LANES : (part + 1) * LANES].T
                table[pl.ds(start + part * LANES, LANES), :] = block.astype(F32)
            return carry

        lax.fori_loop(0, table_rows // span, turn, 0)
        table[pl.ds(table_rows, 8), :] = jnp.zeros((8, LANES), F32)

        unroll = 16
        chunks = owner_rows // unroll

        def look_up(step, carry):
            owner = step // chunks
            source = (owner * 2 + core) * owner_rows + (step % chunks) * unroll
            for part in range(unroll):
                terms = [
                    table[pl.ds(index_ref[slot * group_rows + source + part], 1), :] for slot in range(slots)
                ]
                while len(terms) > 1:
                    terms = [a + b for a, b in zip(terms[::2], terms[1::2])]
                self_row = table[pl.ds(target_ref[source + part], 1), :]
                mean_row = terms[0] / count_ref[source + part].astype(F32)
                rows[pl.ds(step * unroll + part, 1), :] = jnp.where(is_self, self_row, mean_row)
            return carry

        lax.fori_loop(0, owners * chunks, look_up, 0)

        fold = relative_ref.shape[1]
        for owner in range(owners):
            values = rows[pl.ds(owner * owner_rows, owner_rows), :].astype(BF16)
            out_ref[owner] = values[:, : 4 * slice_width]
            turn_y = lax.rem(owner % owners_y - here + owners_y, owners_y)
            for part in range(owner_rows // fold):
                column = (owner // owners_y * (owner_rows // fold) + part) * LANES
                relative_ref[turn_y, :, column : column + LANES] = values[part * fold : (part + 1) * fold]

    smem = pl.BlockSpec(memory_space=pltpu.SMEM)
    vmem = pl.BlockSpec(memory_space=pltpu.VMEM)
    return pl.pallas_call(
        kernel,
        out_shape=(
            jax.ShapeDtypeStruct((owners, owner_rows, 4 * slice_width), BF16),
            jax.ShapeDtypeStruct((owners_y, owners // owners_y * owner_rows * LANES // width, width), BF16),
        ),
        in_specs=[smem, smem, smem, smem, vmem, vmem],
        out_specs=(vmem, vmem),
        scratch_shapes=[
            pltpu.VMEM((table_rows + 8, LANES), F32),
            pltpu.VMEM((owners * owner_rows, LANES), F32),
        ],
        compiler_params=pltpu.CompilerParams(vmem_limit_bytes=30 << 20),
        cost_estimate=pl.CostEstimate(flops=50_000_000, bytes_accessed=100_000_000, transcendentals=0),
        name="gather_mean",
    )


def silu_slope(values):
    sig = jax.nn.sigmoid(values)
    return sig * (1.0 + values * (1.0 - sig))


def swap(values):
    return lax.ppermute(values, "core", [(0, 1), (1, 0)])


def exchange(values, axis):
    return lax.all_to_all(values, axis, split_axis=0, concat_axis=0, tiled=True)


def turn_blocks(blocks, axis):
    n = len(blocks)
    here = lax.axis_index(axis)
    got = [blocks[0]] + [lax.ppermute(blocks[k], axis, [(i, (i + k) % n) for i in range(n)]) for k in range(1, n)]
    return got, lambda got: jnp.stack(
        [lax.dynamic_index_in_dim(jnp.stack(got), (here - j) % n, 0, keepdims=False) for j in range(n)]
    )


def body(
    node_features,
    first_weight,
    second_weight,
    target_nodes,
    outer_nodes,
    outer_counts,
    inner_nodes,
    inner_counts,
    cotangent,
):
    nx, ny, nb = lax.axis_size("x"), lax.axis_size("y"), lax.axis_size("batch")
    core = lax.axis_index("core")
    slice_width, nodes = node_features.shape
    width = second_weight.shape[1]
    half = width // 2
    group_rows, slots = outer_nodes.shape[1:]
    owner_rows = group_rows // (nx * ny * 2)
    second_rows, fan_inner = inner_nodes.shape[1:]
    both = 2 * slice_width
    upstream = cotangent[0]

    weight = first_weight.transpose(1, 0, 2).reshape(both, width)
    weight_mine = exchange(jnp.broadcast_to(weight[None], (nx * ny,) + weight.shape), ("x", "y"))
    weight_mine = weight_mine.reshape(nx * ny * both, width)

    counts = outer_counts[0]
    live = jnp.arange(slots, dtype=jnp.int32)[:, None] < counts[None, :]
    index = jnp.where(live, outer_nodes[0].T, nodes).reshape(-1)
    other_features = swap(node_features)
    stacked, relative = gather_kernel(slots, nx * ny, ny, owner_rows, slice_width, nodes, width)(
        jnp.stack([core, lax.axis_index("y")]).astype(jnp.int32),
        index,
        target_nodes[0],
        counts,
        node_features,
        other_features,
    )
    stacked, weight_mine = lax.optimization_barrier((stacked, weight_mine))
    weight_other, late_upstream = lax.optimization_barrier((swap(weight_mine), upstream))
    owned = exchange(stacked, ("x", "y"))
    owned = owned.reshape(nx * ny, owner_rows, 2, both).transpose(2, 1, 0, 3).reshape(2, owner_rows, nx * ny * both)
    pre = jnp.dot(jnp.where(core == 0, owned[0], owned[1]), weight_mine, preferred_element_type=F32)
    pre += jnp.dot(jnp.where(core == 0, owned[1], owned[0]), weight_other, preferred_element_type=F32)
    hidden = jax.nn.silu(pre).astype(BF16)

    inner = inner_nodes[0]
    inner_cnt = inner_counts[0]
    inner_live = (jnp.arange(fan_inner, dtype=jnp.int32)[None, :] < inner_cnt[:, None]).astype(F32)
    columns = jnp.arange(owner_rows, dtype=jnp.int32)
    tally = jnp.sum((inner[:, :, None] == columns[None, None, :]).astype(F32) * inner_live[:, :, None], axis=1)
    divisor = inner_cnt.astype(F32)[:, None]
    mean_rows = (jnp.dot(tally.astype(BF16), hidden, preferred_element_type=F32) / divisor).astype(BF16)
    joined = jnp.concatenate([hidden[:second_rows], mean_rows], axis=1)
    output = jnp.dot(joined, second_weight, preferred_element_type=F32).astype(BF16)
    grad_joined = lax.dot_general(late_upstream, second_weight, (((1,), (1,)), ((), ())), preferred_element_type=F32)
    spread = lax.dot_general(
        tally, grad_joined[:, width:] / divisor, (((0,), (0,)), ((), ())), precision=lax.Precision.HIGHEST
    )
    grad_hidden = spread + jnp.pad(grad_joined[:, :width], ((0, owner_rows - second_rows), (0, 0)))
    grad_pre = (grad_hidden * silu_slope(pre)).astype(BF16)

    message = jnp.broadcast_to(grad_pre[None], (nx, owner_rows, width))
    columns_y = joined.reshape(second_rows, nx, ny, -1)
    here = lax.axis_index("y")
    folded = second_rows // 2
    pieces = []
    for k in range(ny):
        columns = lax.dynamic_index_in_dim(columns_y, (here + k) % ny, 2, keepdims=False).reshape(second_rows, -1)
        pieces.append(jnp.concatenate([columns[:folded], columns[folded:]], axis=1))
    packed = [jnp.concatenate([pieces[k], upstream, relative[k]], axis=0) for k in range(ny)]
    grad_pre_x = exchange(message, "x").reshape(nx * owner_rows, width)
    packed, in_order = turn_blocks(packed, "y")
    grad_pre_x, packed = lax.optimization_barrier((grad_pre_x, packed))
    along_y = in_order([block[folded + second_rows :] for block in packed])
    along_y = along_y.reshape(ny, -1, width // LANES, LANES).transpose(0, 2, 1, 3)
    along_y = along_y.reshape(ny, nx * owner_rows, LANES)[:, :, : 2 * both]
    packed = jnp.stack(packed)
    columns_y = packed[:, :folded]
    chunk = columns_y.shape[2] // 2
    columns_y = jnp.concatenate([columns_y[:, :, :chunk], columns_y[:, :, chunk:]], axis=1)
    columns_y = columns_y.reshape(ny * second_rows, chunk)
    upstream_y = packed[:, folded : folded + second_rows].reshape(ny * second_rows, width)
    first_terms = lax.dot_general(
        along_y, grad_pre_x, (((1,), (0,)), ((), ())), preferred_element_type=F32
    ).reshape(ny, 2, both, width)

    kept = lax.dynamic_index_in_dim(first_terms, core, 1, keepdims=False)
    sent = swap(lax.dynamic_index_in_dim(first_terms, 1 - core, 1, keepdims=False).astype(BF16))
    piece = width // nb
    first_terms = (kept + sent.astype(F32)).astype(BF16).reshape(ny, both, nb, piece).transpose(0, 2, 1, 3)
    first_terms = first_terms.reshape(ny * nb, both, piece)
    _, columns_y = lax.optimization_barrier((first_terms, columns_y))
    first_terms = exchange(first_terms, ("y", "batch"))
    first_piece = jnp.sum(first_terms.astype(F32), axis=0).astype(BF16)

    second_terms = lax.dot_general(
        columns_y, upstream_y, (((0,), (0,)), ((), ())), preferred_element_type=F32
    ).reshape(nx, 2, -1, width)
    kept = lax.dynamic_index_in_dim(second_terms, core, 1, keepdims=False)
    sent = swap(lax.dynamic_index_in_dim(second_terms, 1 - core, 1, keepdims=False).astype(BF16))
    second_terms = (kept + sent.astype(F32)).astype(BF16)
    here = lax.axis_index("x")
    got, _ = turn_blocks(
        [lax.dynamic_index_in_dim(second_terms, (here + k) % nx, 0, keepdims=False) for k in range(nx)], "x"
    )
    second_terms = sum(block.astype(F32) for block in got).astype(BF16)
    second_terms = second_terms.reshape(nb, -1, nb, piece).transpose(0, 2, 1, 3).reshape(nb, -1, piece)
    message = jnp.concatenate([jnp.broadcast_to(first_piece[None], (nb, both, piece)), second_terms], axis=1)
    message = exchange(message, "batch")
    grad_second = jnp.sum(message[:, both:].astype(F32), axis=0)
    grad_second = grad_second.reshape(nb, -1, piece).transpose(1, 0, 2).reshape(-1, width)
    grad_first = message[:, :both].reshape(nb, 2, slice_width, piece)
    grad_first = grad_first.transpose(2, 1, 0, 3).reshape(slice_width, 2, width)
    return (output[None], grad_second, grad_first.astype(F32))


def solution(mesh):
    feat, batch = mesh.devices.shape
    fine = Mesh(mesh.devices.reshape(4, feat // 8, 2, batch), ("x", "y", "core", "batch"))
    f = ("x", "y", "core")
    in_specs = (
        P(f, None),
        P(f, None, None),
        P(),
        P("batch", None),
        P("batch", None, None),
        P("batch", None),
        P("batch", f, None),
        P("batch", f),
        P("batch", f, None),
    )
    out_specs = (P("batch", f, None), P(("x", "y", "core", "batch"), None), P(f, None, None))
    return jax.shard_map(body, mesh=fine, in_specs=in_specs, out_specs=out_specs, check_vma=False)
```

```python
import jax
import jax.numpy as jnp
from jax import lax
from jax.experimental import pallas as pl
from jax.experimental.pallas import tpu as pltpu
from jax.sharding import Mesh, PartitionSpec as P

BF16 = jnp.bfloat16
F32 = jnp.float32
LANES = 128


def gather_kernel(slots, owners, owners_y, owner_rows, slice_width, table_rows, width):
    def kernel(place_ref, index_ref, target_ref, count_ref, own_ref, other_ref, out_ref, relative_ref, table, rows):
        core, here = place_ref[0], place_ref[1]
        group_rows = owners * 2 * owner_rows
        lane = lax.broadcasted_iota(jnp.int32, (1, LANES), 1)
        is_self = (lane // slice_width) % 2 == 0
        blocks = 16
        span = blocks * LANES
        tail = jnp.zeros((LANES - 4 * slice_width, span), F32)

        def turn(step, carry):
            start = pl.multiple_of(step * span, span)
            own = own_ref[:, pl.ds(start, span)].astype(F32)
            other = other_ref[:, pl.ds(start, span)].astype(F32)
            first = jnp.where(core == 0, own, other)
            second = jnp.where(core == 0, other, own)
            wide = jnp.concatenate([first, first, second, second, tail], axis=0).astype(BF16)
            for part in range(blocks):
                block = wide[:, part * LANES : (part + 1) * LANES].T
                table[pl.ds(start + part * LANES, LANES), :] = block.astype(F32)
            return carry

        lax.fori_loop(0, table_rows // span, turn, 0)
        table[pl.ds(table_rows, 8), :] = jnp.zeros((8, LANES), F32)

        unroll = 16
        chunks = owner_rows // unroll

        def look_up(step, carry):
            owner = step // chunks
            source = (owner * 2 + core) * owner_rows + (step % chunks) * unroll
            for part in range(unroll):
                terms = [
                    table[pl.ds(index_ref[slot * group_rows + source + part], 1), :] for slot in range(slots)
                ]
                while len(terms) > 1:
                    terms = [a + b for a, b in zip(terms[::2], terms[1::2])]
                self_row = table[pl.ds(target_ref[source + part], 1), :]
                mean_row = terms[0] / count_ref[source + part].astype(F32)
                rows[pl.ds(step * unroll + part, 1), :] = jnp.where(is_self, self_row, mean_row)
            return carry

        lax.fori_loop(0, owners * chunks, look_up, 0)

        fold = relative_ref.shape[1]
        for owner in range(owners):
            values = rows[pl.ds(owner * owner_rows, owner_rows), :].astype(BF16)
            out_ref[owner] = values[:, : 4 * slice_width]
            turn_y = lax.rem(owner % owners_y - here + owners_y, owners_y)
            for part in range(owner_rows // fold):
                column = (owner // owners_y * (owner_rows // fold) + part) * LANES
                relative_ref[turn_y, :, column : column + LANES] = values[part * fold : (part + 1) * fold]

    smem = pl.BlockSpec(memory_space=pltpu.SMEM)
    vmem = pl.BlockSpec(memory_space=pltpu.VMEM)
    return pl.pallas_call(
        kernel,
        out_shape=(
            jax.ShapeDtypeStruct((owners, owner_rows, 4 * slice_width), BF16),
            jax.ShapeDtypeStruct((owners_y, owners // owners_y * owner_rows * LANES // width, width), BF16),
        ),
        in_specs=[smem, smem, smem, smem, vmem, vmem],
        out_specs=(vmem, vmem),
        scratch_shapes=[
            pltpu.VMEM((table_rows + 8, LANES), F32),
            pltpu.VMEM((owners * owner_rows, LANES), F32),
        ],
        compiler_params=pltpu.CompilerParams(vmem_limit_bytes=30 << 20),
        cost_estimate=pl.CostEstimate(flops=50_000_000, bytes_accessed=100_000_000, transcendentals=0),
        name="gather_mean",
    )


def owner_kernel(nx, ny, owner_rows, second_rows, fan, width, both):
    def kernel(place_ref, owned_ref, mine_ref, other_ref, inner_ref, count_ref, grad_ref,
               message_ref, joined_ref, columns_ref):
        core, here = place_ref[0], place_ref[1]
        pre = jnp.zeros((owner_rows, width), F32)
        for pair in range(nx * ny):
            rows = owned_ref[pair]
            turned = jnp.concatenate([rows[:, both:], rows[:, :both]], axis=1)
            rows = jnp.where(core == 0, rows, turned)
            weight = jnp.concatenate([mine_ref[pair], other_ref[pair]], axis=0)
            pre += jnp.dot(rows, weight, preferred_element_type=F32)
        sig = jax.nn.sigmoid(pre)
        hidden = (pre * sig).astype(BF16)

        count = count_ref[...]
        row = lax.broadcasted_iota(jnp.int32, (owner_rows, second_rows), 0)
        tally = jnp.zeros((owner_rows, second_rows), F32)
        for slot in range(fan):
            tally += jnp.where(inner_ref[slot : slot + 1, :] == row, 1.0, 0.0)
        tally = tally.astype(BF16)
        diagonal = lax.broadcasted_iota(jnp.int32, (second_rows, second_rows), 0) == lax.broadcasted_iota(
            jnp.int32, (second_rows, second_rows), 1
        )
        divisor = jnp.sum(jnp.where(diagonal, count.astype(F32), 0.0), axis=1, keepdims=True)
        rows_of = (((0,), (0,)), ((), ()))
        mean_rows = lax.dot_general(tally, hidden, rows_of, preferred_element_type=F32) / divisor
        joined_ref[:, :width] = hidden[:second_rows]
        joined_ref[:, width:] = mean_rows.astype(BF16)

        grad_self, grad_mean = grad_ref[:, :width], grad_ref[:, width:]
        rest = grad_mean / divisor
        grad_hidden = jnp.zeros((owner_rows, width), F32)
        for _ in range(3):
            part = rest.astype(BF16)
            rest = rest - part.astype(F32)
            grad_hidden += jnp.dot(tally, part, preferred_element_type=F32)
        grad_hidden = jnp.concatenate(
            [grad_hidden[:second_rows] + grad_self, grad_hidden[second_rows:]], axis=0
        )
        grad_pre = (grad_hidden * (sig * (1.0 + pre * (1.0 - sig)))).astype(BF16)
        for x in range(nx):
            message_ref[x] = grad_pre

        half = second_rows // 2
        for turn in range(ny):
            y = lax.rem(here + turn, ny)
            for x in range(nx):
                columns = joined_ref[:, pl.ds(pl.multiple_of((x * ny + y) * LANES, LANES), LANES)]
                columns_ref[turn, :, x * LANES : (x + 1) * LANES] = columns[:half]
                columns_ref[turn, :, (nx + x) * LANES : (nx + x + 1) * LANES] = columns[half:]

    smem = pl.BlockSpec(memory_space=pltpu.SMEM)
    vmem = pl.BlockSpec(memory_space=pltpu.VMEM)
    return pl.pallas_call(
        kernel,
        out_shape=(
            jax.ShapeDtypeStruct((nx, owner_rows, width), BF16),
            jax.ShapeDtypeStruct((second_rows, 2 * width), BF16),
            jax.ShapeDtypeStruct((ny, second_rows // 2, 2 * nx * LANES), BF16),
        ),
        in_specs=[smem] + [vmem] * 6,
        out_specs=(vmem, vmem, vmem),
        compiler_params=pltpu.CompilerParams(vmem_limit_bytes=24 << 20),
        cost_estimate=pl.CostEstimate(flops=350_000_000, bytes_accessed=9_000_000, transcendentals=65536),
        name="owner_layers",
    )


def swap(values):
    return lax.ppermute(values, "core", [(0, 1), (1, 0)])


def exchange(values, axis):
    return lax.all_to_all(values, axis, split_axis=0, concat_axis=0, tiled=True)


def turn_blocks(blocks, axis):
    n = len(blocks)
    here = lax.axis_index(axis)
    got = [blocks[0]] + [lax.ppermute(blocks[k], axis, [(i, (i + k) % n) for i in range(n)]) for k in range(1, n)]
    return got, lambda got: jnp.stack(
        [lax.dynamic_index_in_dim(jnp.stack(got), (here - j) % n, 0, keepdims=False) for j in range(n)]
    )


def body(
    node_features,
    first_weight,
    second_weight,
    target_nodes,
    outer_nodes,
    outer_counts,
    inner_nodes,
    inner_counts,
    cotangent,
):
    nx, ny, nb = lax.axis_size("x"), lax.axis_size("y"), lax.axis_size("batch")
    core = lax.axis_index("core")
    place = jnp.stack([core, lax.axis_index("y")]).astype(jnp.int32)
    slice_width, nodes = node_features.shape
    width = second_weight.shape[1]
    half = width // 2
    group_rows, slots = outer_nodes.shape[1:]
    owner_rows = group_rows // (nx * ny * 2)
    second_rows, fan_inner = inner_nodes.shape[1:]
    both = 2 * slice_width
    upstream = cotangent[0]

    weight = first_weight.transpose(1, 0, 2).reshape(both, width)
    weight_mine = exchange(jnp.broadcast_to(weight[None], (nx * ny,) + weight.shape), ("x", "y"))

    counts = outer_counts[0]
    live = jnp.arange(slots, dtype=jnp.int32)[:, None] < counts[None, :]
    index = jnp.where(live, outer_nodes[0].T, nodes).reshape(-1)
    other_features = swap(node_features)
    stacked, relative = gather_kernel(slots, nx * ny, ny, owner_rows, slice_width, nodes, width)(
        place,
        index,
        target_nodes[0],
        counts,
        node_features,
        other_features,
    )
    stacked, weight_mine = lax.optimization_barrier((stacked, weight_mine))
    weight_other = swap(weight_mine)
    _, late_upstream, inner, inner_count = lax.optimization_barrier(
        (relative, upstream, inner_nodes[0].T, inner_counts)
    )
    grad_joined = lax.dot_general(late_upstream, second_weight, (((1,), (1,)), ((), ())), preferred_element_type=F32)
    inner = jnp.where(jnp.arange(fan_inner, dtype=jnp.int32)[:, None] < inner_count, inner, owner_rows)
    owned = exchange(stacked, ("x", "y"))
    message, joined, pieces = owner_kernel(nx, ny, owner_rows, second_rows, fan_inner, width, both)(
        place, owned, weight_mine, weight_other, inner, inner_counts, grad_joined
    )
    output = jnp.dot(joined, second_weight, preferred_element_type=F32).astype(BF16)
    folded = second_rows // 2
    packed = [jnp.concatenate([pieces[k], upstream, relative[k]], axis=0) for k in range(ny)]
    grad_pre_x = exchange(message, "x").reshape(nx * owner_rows, width)
    packed, in_order = turn_blocks(packed, "y")
    grad_pre_x, packed = lax.optimization_barrier((grad_pre_x, packed))
    along_y = in_order([block[folded + second_rows :] for block in packed])
    along_y = along_y.reshape(ny, -1, width // LANES, LANES).transpose(0, 2, 1, 3)
    along_y = along_y.reshape(ny, nx * owner_rows, LANES)[:, :, : 2 * both]
    packed = jnp.stack(packed)
    columns_y = packed[:, :folded]
    chunk = columns_y.shape[2] // 2
    columns_y = jnp.concatenate([columns_y[:, :, :chunk], columns_y[:, :, chunk:]], axis=1)
    columns_y = columns_y.reshape(ny * second_rows, chunk)
    upstream_y = packed[:, folded : folded + second_rows].reshape(ny * second_rows, width)
    first_terms = lax.dot_general(
        along_y, grad_pre_x, (((1,), (0,)), ((), ())), preferred_element_type=F32
    ).reshape(ny, 2, both, width)

    kept = lax.dynamic_index_in_dim(first_terms, core, 1, keepdims=False)
    sent = swap(lax.dynamic_index_in_dim(first_terms, 1 - core, 1, keepdims=False).astype(BF16))
    piece = width // nb
    first_terms = (kept + sent.astype(F32)).astype(BF16).reshape(ny, both, nb, piece).transpose(0, 2, 1, 3)
    first_terms = first_terms.reshape(ny * nb, both, piece)
    _, columns_y = lax.optimization_barrier((first_terms, columns_y))
    first_terms = exchange(first_terms, ("y", "batch"))
    first_piece = jnp.sum(first_terms.astype(F32), axis=0).astype(BF16)

    second_terms = lax.dot_general(
        columns_y, upstream_y, (((0,), (0,)), ((), ())), preferred_element_type=F32
    ).reshape(nx, 2, -1, width)
    kept = lax.dynamic_index_in_dim(second_terms, core, 1, keepdims=False)
    sent = swap(lax.dynamic_index_in_dim(second_terms, 1 - core, 1, keepdims=False).astype(BF16))
    second_terms = (kept + sent.astype(F32)).astype(BF16)
    here = lax.axis_index("x")
    got, _ = turn_blocks(
        [lax.dynamic_index_in_dim(second_terms, (here + k) % nx, 0, keepdims=False) for k in range(nx)], "x"
    )
    second_terms = sum(block.astype(F32) for block in got).astype(BF16)
    second_terms = second_terms.reshape(nb, -1, nb, piece).transpose(0, 2, 1, 3).reshape(nb, -1, piece)
    message = jnp.concatenate([jnp.broadcast_to(first_piece[None], (nb, both, piece)), second_terms], axis=1)
    message = exchange(message, "batch")
    grad_second = jnp.sum(message[:, both:].astype(F32), axis=0)
    grad_second = grad_second.reshape(nb, -1, piece).transpose(1, 0, 2).reshape(-1, width)
    grad_first = message[:, :both].reshape(nb, 2, slice_width, piece)
    grad_first = grad_first.transpose(2, 1, 0, 3).reshape(slice_width, 2, width)
    return (output[None], grad_second, grad_first.astype(F32))


def solution(mesh):
    feat, batch = mesh.devices.shape
    fine = Mesh(mesh.devices.reshape(4, feat // 8, 2, batch), ("x", "y", "core", "batch"))
    f = ("x", "y", "core")
    in_specs = (
        P(f, None),
        P(f, None, None),
        P(),
        P("batch", None),
        P("batch", None, None),
        P("batch", None),
        P("batch", f, None),
        P("batch", f),
        P("batch", f, None),
    )
    out_specs = (P("batch", f, None), P(("x", "y", "core", "batch"), None), P(f, None, None))
    return jax.shard_map(body, mesh=fine, in_specs=in_specs, out_specs=out_specs, check_vma=False)
```

```python
import jax
import jax.numpy as jnp
from jax import lax
from jax.experimental import pallas as pl
from jax.experimental.pallas import tpu as pltpu
from jax.sharding import Mesh, PartitionSpec as P

BF16 = jnp.bfloat16
F32 = jnp.float32
LANES = 128


def gather_kernel(slots, owners, owners_y, owner_rows, slice_width, table_rows, width):
    def kernel(place_ref, index_ref, target_ref, count_ref, own_ref, other_ref, out_ref, relative_ref, table, rows):
        core, here = place_ref[0], place_ref[1]
        group_rows = owners * 2 * owner_rows
        lane = lax.broadcasted_iota(jnp.int32, (1, LANES), 1)
        is_self = (lane // slice_width) % 2 == 0
        blocks = 16
        span = blocks * LANES
        tail = jnp.zeros((LANES - 4 * slice_width, span), F32)

        def turn(step, carry):
            start = pl.multiple_of(step * span, span)
            own = own_ref[:, pl.ds(start, span)].astype(F32)
            other = other_ref[:, pl.ds(start, span)].astype(F32)
            first = jnp.where(core == 0, own, other)
            second = jnp.where(core == 0, other, own)
            wide = jnp.concatenate([first, first, second, second, tail], axis=0).astype(BF16)
            for part in range(blocks):
                block = wide[:, part * LANES : (part + 1) * LANES].T
                table[pl.ds(start + part * LANES, LANES), :] = block.astype(F32)
            return carry

        lax.fori_loop(0, table_rows // span, turn, 0)
        table[pl.ds(table_rows, 8), :] = jnp.zeros((8, LANES), F32)

        unroll = 16
        chunks = owner_rows // unroll

        def look_up(step, carry):
            owner = step // chunks
            source = (owner * 2 + core) * owner_rows + (step % chunks) * unroll
            for part in range(unroll):
                terms = [
                    table[pl.ds(index_ref[slot * group_rows + source + part], 1), :] for slot in range(slots)
                ]
                while len(terms) > 1:
                    terms = [a + b for a, b in zip(terms[::2], terms[1::2])]
                self_row = table[pl.ds(target_ref[source + part], 1), :]
                mean_row = terms[0] / count_ref[source + part].astype(F32)
                rows[pl.ds(step * unroll + part, 1), :] = jnp.where(is_self, self_row, mean_row)
            return carry

        lax.fori_loop(0, owners * chunks, look_up, 0)

        fold = relative_ref.shape[1]
        for owner in range(owners):
            values = rows[pl.ds(owner * owner_rows, owner_rows), :].astype(BF16)
            out_ref[owner] = values[:, : 4 * slice_width]
            turn_y = lax.rem(owner % owners_y - here + owners_y, owners_y)
            for part in range(owner_rows // fold):
                column = (owner // owners_y * (owner_rows // fold) + part) * LANES
                relative_ref[turn_y, :, column : column + LANES] = values[part * fold : (part + 1) * fold]

    smem = pl.BlockSpec(memory_space=pltpu.SMEM)
    vmem = pl.BlockSpec(memory_space=pltpu.VMEM)
    return pl.pallas_call(
        kernel,
        out_shape=(
            jax.ShapeDtypeStruct((owners, owner_rows, 4 * slice_width), BF16),
            jax.ShapeDtypeStruct((owners_y, owners // owners_y * owner_rows * LANES // width, width), BF16),
        ),
        in_specs=[smem, smem, smem, smem, vmem, vmem],
        out_specs=(vmem, vmem),
        scratch_shapes=[
            pltpu.VMEM((table_rows + 8, LANES), F32),
            pltpu.VMEM((owners * owner_rows, LANES), F32),
        ],
        compiler_params=pltpu.CompilerParams(vmem_limit_bytes=30 << 20),
        cost_estimate=pl.CostEstimate(flops=50_000_000, bytes_accessed=100_000_000, transcendentals=0),
        name="gather_mean",
    )


def owner_kernel(nx, ny, owner_rows, second_rows, fan, width, both):
    def kernel(place_ref, owned_ref, mine_ref, other_ref, inner_ref, count_ref, grad_ref,
               message_ref, joined_ref, columns_ref):
        core, here = place_ref[0], place_ref[1]
        pre = jnp.zeros((owner_rows, width), F32)
        for pair in range(nx * ny):
            rows = owned_ref[pair]
            turned = jnp.concatenate([rows[:, both:], rows[:, :both]], axis=1)
            rows = jnp.where(core == 0, rows, turned)
            weight = jnp.concatenate([mine_ref[pair], other_ref[pair]], axis=0)
            pre += jnp.dot(rows, weight, preferred_element_type=F32)
        sig = jax.nn.sigmoid(pre)
        hidden = (pre * sig).astype(BF16)

        count = count_ref[...]
        row = lax.broadcasted_iota(jnp.int32, (owner_rows, second_rows), 0)
        tally = jnp.zeros((owner_rows, second_rows), F32)
        for slot in range(fan):
            tally += jnp.where(inner_ref[slot : slot + 1, :] == row, 1.0, 0.0)
        tally = tally.astype(BF16)
        diagonal = lax.broadcasted_iota(jnp.int32, (second_rows, second_rows), 0) == lax.broadcasted_iota(
            jnp.int32, (second_rows, second_rows), 1
        )
        divisor = jnp.sum(jnp.where(diagonal, count.astype(F32), 0.0), axis=1, keepdims=True)
        rows_of = (((0,), (0,)), ((), ()))
        mean_rows = lax.dot_general(tally, hidden, rows_of, preferred_element_type=F32) / divisor
        joined_ref[:, :width] = hidden[:second_rows]
        joined_ref[:, width:] = mean_rows.astype(BF16)

        grad_self, grad_mean = grad_ref[:, :width], grad_ref[:, width:]
        rest = grad_mean / divisor
        grad_hidden = jnp.zeros((owner_rows, width), F32)
        for _ in range(3):
            part = rest.astype(BF16)
            rest = rest - part.astype(F32)
            grad_hidden += jnp.dot(tally, part, preferred_element_type=F32)
        grad_hidden = jnp.concatenate(
            [grad_hidden[:second_rows] + grad_self, grad_hidden[second_rows:]], axis=0
        )
        grad_pre = (grad_hidden * (sig * (1.0 + pre * (1.0 - sig)))).astype(BF16)
        for x in range(nx):
            message_ref[x] = grad_pre

        half = second_rows // 2
        for turn in range(ny):
            y = lax.rem(here + turn, ny)
            for x in range(nx):
                columns = joined_ref[:, pl.ds(pl.multiple_of((x * ny + y) * LANES, LANES), LANES)]
                columns_ref[turn, :, x * LANES : (x + 1) * LANES] = columns[:half]
                columns_ref[turn, :, (nx + x) * LANES : (nx + x + 1) * LANES] = columns[half:]

    smem = pl.BlockSpec(memory_space=pltpu.SMEM)
    vmem = pl.BlockSpec(memory_space=pltpu.VMEM)
    return pl.pallas_call(
        kernel,
        out_shape=(
            jax.ShapeDtypeStruct((nx, owner_rows, width), BF16),
            jax.ShapeDtypeStruct((second_rows, 2 * width), BF16),
            jax.ShapeDtypeStruct((ny, second_rows // 2, 2 * nx * LANES), BF16),
        ),
        in_specs=[smem] + [vmem] * 6,
        out_specs=(vmem, vmem, vmem),
        compiler_params=pltpu.CompilerParams(vmem_limit_bytes=24 << 20),
        cost_estimate=pl.CostEstimate(flops=350_000_000, bytes_accessed=9_000_000, transcendentals=65536),
        name="owner_layers",
    )


def swap(values):
    return lax.ppermute(values, "core", [(0, 1), (1, 0)])


def exchange(values, axis):
    return lax.all_to_all(values, axis, split_axis=0, concat_axis=0, tiled=True)


def turn_blocks(blocks, axis):
    n = len(blocks)
    here = lax.axis_index(axis)
    got = [blocks[0]] + [lax.ppermute(blocks[k], axis, [(i, (i + k) % n) for i in range(n)]) for k in range(1, n)]
    return got, lambda got: jnp.stack(
        [lax.dynamic_index_in_dim(jnp.stack(got), (here - j) % n, 0, keepdims=False) for j in range(n)]
    )


def body(
    node_features,
    first_weight,
    second_weight,
    target_nodes,
    outer_nodes,
    outer_counts,
    inner_nodes,
    inner_counts,
    cotangent,
):
    nx, ny, nb = lax.axis_size("x"), lax.axis_size("y"), lax.axis_size("batch")
    core = lax.axis_index("core")
    place = jnp.stack([core, lax.axis_index("y")]).astype(jnp.int32)
    slice_width, nodes = node_features.shape
    width = second_weight.shape[1]
    half = width // 2
    group_rows, slots = outer_nodes.shape[1:]
    owner_rows = group_rows // (nx * ny * 2)
    second_rows, fan_inner = inner_nodes.shape[1:]
    both = 2 * slice_width
    upstream = cotangent[0]

    weight = first_weight.transpose(1, 0, 2).reshape(both, width)
    weight_mine = exchange(jnp.broadcast_to(weight[None], (nx * ny,) + weight.shape), ("x", "y"))

    counts = outer_counts[0]
    live = jnp.arange(slots, dtype=jnp.int32)[:, None] < counts[None, :]
    index = jnp.where(live, outer_nodes[0].T, nodes).reshape(-1)
    other_features = swap(node_features)
    stacked, relative = gather_kernel(slots, nx * ny, ny, owner_rows, slice_width, nodes, width)(
        place,
        index,
        target_nodes[0],
        counts,
        node_features,
        other_features,
    )
    stacked, weight_mine = lax.optimization_barrier((stacked, weight_mine))
    weight_other = swap(weight_mine)
    _, late_upstream, inner, inner_count = lax.optimization_barrier(
        (relative, upstream, inner_nodes[0].T, inner_counts)
    )
    grad_joined = lax.dot_general(late_upstream, second_weight, (((1,), (1,)), ((), ())), preferred_element_type=F32)
    inner = jnp.where(jnp.arange(fan_inner, dtype=jnp.int32)[:, None] < inner_count, inner, owner_rows)
    owned = exchange(stacked, ("x", "y"))
    far = ny // 2
    upstream_far = lax.ppermute(upstream, "y", [(i, (i + far) % ny) for i in range(ny)])
    owned, upstream_far = lax.optimization_barrier((owned, upstream_far))
    message, joined, pieces = owner_kernel(nx, ny, owner_rows, second_rows, fan_inner, width, both)(
        place, owned, weight_mine, weight_other, inner, inner_counts, grad_joined
    )
    output = jnp.dot(joined, second_weight, preferred_element_type=F32).astype(BF16)
    folded = second_rows // 2
    packed = [
        jnp.concatenate([pieces[k], relative[k]] + [upstream] * (k != far), axis=0) for k in range(ny)
    ]
    grad_pre_x = exchange(message, "x").reshape(nx * owner_rows, width)
    packed, in_order = turn_blocks(packed, "y")
    grad_pre_x, packed = lax.optimization_barrier((grad_pre_x, packed))
    turned = folded + relative.shape[1]
    along_y = in_order([block[folded:turned] for block in packed])
    along_y = along_y.reshape(ny, -1, width // LANES, LANES).transpose(0, 2, 1, 3)
    along_y = along_y.reshape(ny, nx * owner_rows, LANES)[:, :, : 2 * both]
    columns_y = jnp.stack([block[:folded] for block in packed])
    chunk = columns_y.shape[2] // 2
    columns_y = jnp.concatenate([columns_y[:, :, :chunk], columns_y[:, :, chunk:]], axis=1)
    columns_y = columns_y.reshape(ny * second_rows, chunk)
    upstream_y = jnp.concatenate([upstream_far if k == far else packed[k][turned:] for k in range(ny)], axis=0)
    first_terms = lax.dot_general(
        along_y, grad_pre_x, (((1,), (0,)), ((), ())), preferred_element_type=F32
    ).reshape(ny, 2, both, width)

    kept = lax.dynamic_index_in_dim(first_terms, core, 1, keepdims=False)
    sent = swap(lax.dynamic_index_in_dim(first_terms, 1 - core, 1, keepdims=False).astype(BF16))
    piece = width // nb
    first_terms = (kept + sent.astype(F32)).astype(BF16).reshape(ny, both, nb, piece).transpose(0, 2, 1, 3)
    first_terms = first_terms.reshape(ny * nb, both, piece)
    _, columns_y = lax.optimization_barrier((first_terms, columns_y))
    first_terms = exchange(first_terms, ("y", "batch"))
    first_piece = jnp.sum(first_terms.astype(F32), axis=0).astype(BF16)

    second_terms = lax.dot_general(
        columns_y, upstream_y, (((0,), (0,)), ((), ())), preferred_element_type=F32
    ).reshape(nx, 2, -1, width)
    kept = lax.dynamic_index_in_dim(second_terms, core, 1, keepdims=False)
    sent = swap(lax.dynamic_index_in_dim(second_terms, 1 - core, 1, keepdims=False).astype(BF16))
    second_terms = (kept + sent.astype(F32)).astype(BF16)
    here = lax.axis_index("x")
    got, _ = turn_blocks(
        [lax.dynamic_index_in_dim(second_terms, (here + k) % nx, 0, keepdims=False) for k in range(nx)], "x"
    )
    second_terms = sum(block.astype(F32) for block in got).astype(BF16)
    second_terms = second_terms.reshape(nb, -1, nb, piece).transpose(0, 2, 1, 3).reshape(nb, -1, piece)
    message = jnp.concatenate([jnp.broadcast_to(first_piece[None], (nb, both, piece)), second_terms], axis=1)
    message = exchange(message, "batch")
    grad_second = jnp.sum(message[:, both:].astype(F32), axis=0)
    grad_second = grad_second.reshape(nb, -1, piece).transpose(1, 0, 2).reshape(-1, width)
    grad_first = message[:, :both].reshape(nb, 2, slice_width, piece)
    grad_first = grad_first.transpose(2, 1, 0, 3).reshape(slice_width, 2, width)
    return (output[None], grad_second, grad_first.astype(F32))


def solution(mesh):
    feat, batch = mesh.devices.shape
    fine = Mesh(mesh.devices.reshape(4, feat // 8, 2, batch), ("x", "y", "core", "batch"))
    f = ("x", "y", "core")
    in_specs = (
        P(f, None),
        P(f, None, None),
        P(),
        P("batch", None),
        P("batch", None, None),
        P("batch", None),
        P("batch", f, None),
        P("batch", f),
        P("batch", f, None),
    )
    out_specs = (P("batch", f, None), P(("x", "y", "core", "batch"), None), P(f, None, None))
    return jax.shard_map(body, mesh=fine, in_specs=in_specs, out_specs=out_specs, check_vma=False)
```

```python
import jax
import jax.numpy as jnp
from jax import lax
from jax.experimental import pallas as pl
from jax.experimental.pallas import tpu as pltpu
from jax.sharding import Mesh, PartitionSpec as P

BF16 = jnp.bfloat16
F32 = jnp.float32
LANES = 128


def gather_kernel(slots, owners, owners_y, owner_rows, slice_width, table_rows, width):
    def kernel(place_ref, index_ref, target_ref, count_ref, own_ref, other_ref, out_ref, relative_ref, table, rows):
        core, here = place_ref[0], place_ref[1]
        group_rows = owners * 2 * owner_rows
        lane = lax.broadcasted_iota(jnp.int32, (1, LANES), 1)
        is_self = (lane // slice_width) % 2 == 0
        blocks = 16
        span = blocks * LANES
        tail = jnp.zeros((LANES - 4 * slice_width, span), F32)

        def turn(step, carry):
            start = pl.multiple_of(step * span, span)
            own = own_ref[:, pl.ds(start, span)].astype(F32)
            other = other_ref[:, pl.ds(start, span)].astype(F32)
            first = jnp.where(core == 0, own, other)
            second = jnp.where(core == 0, other, own)
            wide = jnp.concatenate([first, first, second, second, tail], axis=0).astype(BF16)
            for part in range(blocks):
                block = wide[:, part * LANES : (part + 1) * LANES].T
                table[pl.ds(start + part * LANES, LANES), :] = block.astype(F32)
            return carry

        lax.fori_loop(0, table_rows // span, turn, 0)
        table[pl.ds(table_rows, 8), :] = jnp.zeros((8, LANES), F32)

        unroll = 16
        chunks = owner_rows // unroll

        def look_up(step, carry):
            owner = step // chunks
            source = (owner * 2 + core) * owner_rows + (step % chunks) * unroll
            for part in range(unroll):
                terms = [
                    table[pl.ds(index_ref[slot * group_rows + source + part], 1), :] for slot in range(slots)
                ]
                while len(terms) > 1:
                    terms = [a + b for a, b in zip(terms[::2], terms[1::2])]
                self_row = table[pl.ds(target_ref[source + part], 1), :]
                mean_row = terms[0] / count_ref[source + part].astype(F32)
                rows[pl.ds(step * unroll + part, 1), :] = jnp.where(is_self, self_row, mean_row)
            return carry

        lax.fori_loop(0, owners * chunks, look_up, 0)

        fold = relative_ref.shape[1]
        for owner in range(owners):
            values = rows[pl.ds(owner * owner_rows, owner_rows), :].astype(BF16)
            out_ref[owner] = values[:, : 4 * slice_width]
            turn_y = lax.rem(owner % owners_y - here + owners_y, owners_y)
            for part in range(owner_rows // fold):
                column = (owner // owners_y * (owner_rows // fold) + part) * LANES
                relative_ref[turn_y, :, column : column + LANES] = values[part * fold : (part + 1) * fold]

    smem = pl.BlockSpec(memory_space=pltpu.SMEM)
    vmem = pl.BlockSpec(memory_space=pltpu.VMEM)
    return pl.pallas_call(
        kernel,
        out_shape=(
            jax.ShapeDtypeStruct((owners, owner_rows, 4 * slice_width), BF16),
            jax.ShapeDtypeStruct((owners_y, owners // owners_y * owner_rows * LANES // width, width), BF16),
        ),
        in_specs=[smem, smem, smem, smem, vmem, vmem],
        out_specs=(vmem, vmem),
        scratch_shapes=[
            pltpu.VMEM((table_rows + 8, LANES), F32),
            pltpu.VMEM((owners * owner_rows, LANES), F32),
        ],
        compiler_params=pltpu.CompilerParams(vmem_limit_bytes=30 << 20),
        cost_estimate=pl.CostEstimate(flops=50_000_000, bytes_accessed=100_000_000, transcendentals=0),
        name="gather_mean",
    )


def owner_kernel(nx, ny, owner_rows, second_rows, fan, width, both):
    def kernel(place_ref, owned_ref, mine_ref, other_ref, inner_ref, count_ref, grad_ref,
               message_ref, joined_ref, columns_ref):
        core, here = place_ref[0], place_ref[1]
        pre = jnp.zeros((owner_rows, width), F32)
        for pair in range(nx * ny):
            rows = owned_ref[pair]
            turned = jnp.concatenate([rows[:, both:], rows[:, :both]], axis=1)
            rows = jnp.where(core == 0, rows, turned)
            weight = jnp.concatenate([mine_ref[pair], other_ref[pair]], axis=0)
            pre += jnp.dot(rows, weight, preferred_element_type=F32)
        sig = jax.nn.sigmoid(pre)
        hidden = (pre * sig).astype(BF16)

        count = count_ref[...]
        row = lax.broadcasted_iota(jnp.int32, (owner_rows, second_rows), 0)
        tally = jnp.zeros((owner_rows, second_rows), F32)
        for slot in range(fan):
            tally += jnp.where(inner_ref[slot : slot + 1, :] == row, 1.0, 0.0)
        tally = tally.astype(BF16)
        diagonal = lax.broadcasted_iota(jnp.int32, (second_rows, second_rows), 0) == lax.broadcasted_iota(
            jnp.int32, (second_rows, second_rows), 1
        )
        divisor = jnp.sum(jnp.where(diagonal, count.astype(F32), 0.0), axis=1, keepdims=True)
        rows_of = (((0,), (0,)), ((), ()))
        mean_rows = lax.dot_general(tally, hidden, rows_of, preferred_element_type=F32) / divisor
        joined_ref[:, :width] = hidden[:second_rows]
        joined_ref[:, width:] = mean_rows.astype(BF16)

        grad_self, grad_mean = grad_ref[:, :width], grad_ref[:, width:]
        rest = grad_mean / divisor
        grad_hidden = jnp.zeros((owner_rows, width), F32)
        for _ in range(3):
            part = rest.astype(BF16)
            rest = rest - part.astype(F32)
            grad_hidden += jnp.dot(tally, part, preferred_element_type=F32)
        grad_hidden = jnp.concatenate(
            [grad_hidden[:second_rows] + grad_self, grad_hidden[second_rows:]], axis=0
        )
        grad_pre = (grad_hidden * (sig * (1.0 + pre * (1.0 - sig)))).astype(BF16)
        for x in range(nx):
            message_ref[x] = grad_pre

        half = second_rows // 2
        for turn in range(ny):
            y = lax.rem(here + turn, ny)
            for x in range(nx):
                columns = joined_ref[:, pl.ds(pl.multiple_of((x * ny + y) * LANES, LANES), LANES)]
                columns_ref[turn, :, x * LANES : (x + 1) * LANES] = columns[:half]
                columns_ref[turn, :, (nx + x) * LANES : (nx + x + 1) * LANES] = columns[half:]

    smem = pl.BlockSpec(memory_space=pltpu.SMEM)
    vmem = pl.BlockSpec(memory_space=pltpu.VMEM)
    return pl.pallas_call(
        kernel,
        out_shape=(
            jax.ShapeDtypeStruct((nx, owner_rows, width), BF16),
            jax.ShapeDtypeStruct((second_rows, 2 * width), BF16),
            jax.ShapeDtypeStruct((ny, second_rows // 2, 2 * nx * LANES), BF16),
        ),
        in_specs=[smem] + [vmem] * 6,
        out_specs=(vmem, vmem, vmem),
        compiler_params=pltpu.CompilerParams(vmem_limit_bytes=24 << 20),
        cost_estimate=pl.CostEstimate(flops=350_000_000, bytes_accessed=9_000_000, transcendentals=65536),
        name="owner_layers",
    )


def swap(values):
    return lax.ppermute(values, "core", [(0, 1), (1, 0)])


def exchange(values, axis):
    return lax.all_to_all(values, axis, split_axis=0, concat_axis=0, tiled=True)


def turn_blocks(blocks, axis):
    n = len(blocks)
    here = lax.axis_index(axis)
    got = [blocks[0]] + [lax.ppermute(blocks[k], axis, [(i, (i + k) % n) for i in range(n)]) for k in range(1, n)]
    return got, lambda got: jnp.stack(
        [lax.dynamic_index_in_dim(jnp.stack(got), (here - j) % n, 0, keepdims=False) for j in range(n)]
    )


def body(
    node_features,
    first_weight,
    second_weight,
    target_nodes,
    outer_nodes,
    outer_counts,
    inner_nodes,
    inner_counts,
    cotangent,
):
    nx, ny, nb = lax.axis_size("x"), lax.axis_size("y"), lax.axis_size("batch")
    core = lax.axis_index("core")
    place = jnp.stack([core, lax.axis_index("y")]).astype(jnp.int32)
    slice_width, nodes = node_features.shape
    width = second_weight.shape[1]
    half = width // 2
    group_rows, slots = outer_nodes.shape[1:]
    owner_rows = group_rows // (nx * ny * 2)
    second_rows, fan_inner = inner_nodes.shape[1:]
    both = 2 * slice_width
    upstream = cotangent[0]

    weight_mine = exchange(jnp.broadcast_to(first_weight[None], (nx * ny,) + first_weight.shape), ("x", "y"))

    counts = outer_counts[0]
    live = jnp.arange(slots, dtype=jnp.int32)[:, None] < counts[None, :]
    index = jnp.where(live, outer_nodes[0].T, nodes).reshape(-1)
    other_features = swap(node_features)
    stacked, relative = gather_kernel(slots, nx * ny, ny, owner_rows, slice_width, nodes, width)(
        place,
        index,
        target_nodes[0],
        counts,
        node_features,
        other_features,
    )
    stacked, weight_mine = lax.optimization_barrier((stacked, weight_mine))
    weight_mine = weight_mine.transpose(0, 2, 1, 3).reshape(nx * ny, both, width)
    weight_other = swap(weight_mine)
    _, late_upstream, inner, inner_count = lax.optimization_barrier(
        (relative, upstream, inner_nodes[0].T, inner_counts)
    )
    grad_joined = lax.dot_general(late_upstream, second_weight, (((1,), (1,)), ((), ())), preferred_element_type=F32)
    inner = jnp.where(jnp.arange(fan_inner, dtype=jnp.int32)[:, None] < inner_count, inner, owner_rows)
    owned = exchange(stacked, ("x", "y"))
    far = ny // 2
    upstream_far = lax.ppermute(upstream, "y", [(i, (i + far) % ny) for i in range(ny)])
    owned, upstream_far = lax.optimization_barrier((owned, upstream_far))
    message, joined, pieces = owner_kernel(nx, ny, owner_rows, second_rows, fan_inner, width, both)(
        place, owned, weight_mine, weight_other, inner, inner_counts, grad_joined
    )
    output = jnp.dot(joined, second_weight, preferred_element_type=F32).astype(BF16)
    folded = second_rows // 2
    packed = [
        jnp.concatenate([pieces[k], relative[k]] + [upstream] * (k != far), axis=0) for k in range(ny)
    ]
    grad_pre_x = exchange(message, "x").reshape(nx * owner_rows, width)
    packed, in_order = turn_blocks(packed, "y")
    grad_pre_x, packed = lax.optimization_barrier((grad_pre_x, packed))
    turned = folded + relative.shape[1]
    along_y = in_order([block[folded:turned] for block in packed])
    along_y = along_y.reshape(ny, -1, width // LANES, LANES).transpose(0, 2, 1, 3)
    along_y = along_y.reshape(ny, nx * owner_rows, LANES)[:, :, : 2 * both]
    columns_y = jnp.stack([block[:folded] for block in packed])
    chunk = columns_y.shape[2] // 2
    columns_y = jnp.concatenate([columns_y[:, :, :chunk], columns_y[:, :, chunk:]], axis=1)
    columns_y = columns_y.reshape(ny * second_rows, chunk)
    upstream_y = jnp.concatenate([upstream_far if k == far else packed[k][turned:] for k in range(ny)], axis=0)
    first_terms = lax.dot_general(
        along_y, grad_pre_x, (((1,), (0,)), ((), ())), preferred_element_type=F32
    ).reshape(ny, 2, both, width)

    kept = lax.dynamic_index_in_dim(first_terms, core, 1, keepdims=False)
    sent = swap(lax.dynamic_index_in_dim(first_terms, 1 - core, 1, keepdims=False).astype(BF16))
    piece = width // nb
    first_terms = (kept + sent.astype(F32)).astype(BF16).reshape(ny, both, nb, piece).transpose(0, 2, 1, 3)
    first_terms = first_terms.reshape(ny * nb, both, piece)
    _, columns_y = lax.optimization_barrier((first_terms, columns_y))
    first_terms = exchange(first_terms, ("y", "batch"))
    first_piece = jnp.sum(first_terms.astype(F32), axis=0).astype(BF16)

    second_terms = lax.dot_general(
        columns_y, upstream_y, (((0,), (0,)), ((), ())), preferred_element_type=F32
    ).reshape(nx, 2, -1, width)
    kept = lax.dynamic_index_in_dim(second_terms, core, 1, keepdims=False)
    sent = swap(lax.dynamic_index_in_dim(second_terms, 1 - core, 1, keepdims=False).astype(BF16))
    second_terms = (kept + sent.astype(F32)).astype(BF16)
    here = lax.axis_index("x")
    got, _ = turn_blocks(
        [lax.dynamic_index_in_dim(second_terms, (here + k) % nx, 0, keepdims=False) for k in range(nx)], "x"
    )
    second_terms = sum(block.astype(F32) for block in got).astype(BF16)
    second_terms = second_terms.reshape(nb, -1, nb, piece).transpose(0, 2, 1, 3).reshape(nb, -1, piece)
    message = jnp.concatenate([jnp.broadcast_to(first_piece[None], (nb, both, piece)), second_terms], axis=1)
    message = exchange(message, "batch")
    grad_second = jnp.sum(message[:, both:].astype(F32), axis=0)
    grad_second = grad_second.reshape(nb, -1, piece).transpose(1, 0, 2).reshape(-1, width)
    grad_first = message[:, :both].reshape(nb, 2, slice_width, piece)
    grad_first = grad_first.transpose(2, 1, 0, 3).reshape(slice_width, 2, width)
    return (output[None], grad_second, grad_first.astype(F32))


def solution(mesh):
    feat, batch = mesh.devices.shape
    fine = Mesh(mesh.devices.reshape(4, feat // 8, 2, batch), ("x", "y", "core", "batch"))
    f = ("x", "y", "core")
    in_specs = (
        P(f, None),
        P(f, None, None),
        P(),
        P("batch", None),
        P("batch", None, None),
        P("batch", None),
        P("batch", f, None),
        P("batch", f),
        P("batch", f, None),
    )
    out_specs = (P("batch", f, None), P(("x", "y", "core", "batch"), None), P(f, None, None))
    return jax.shard_map(body, mesh=fine, in_specs=in_specs, out_specs=out_specs, check_vma=False)
```
